256 devices in a mesh: blk: 64 (over y, z, core), shard: 4 (over x).
Axes of the slice: x: 4, y: 4, z: 8, core: 2. Of those that a mesh axis runs over, the one named last changes fastest.
Arguments:
- gradient: float32 [64, 1024, 1024], P(None, ('shard', 'blk')), may hold values from -55 to 55
- owner_table: int32 [64], replicated, may hold values from 0 to 63, each once
- restart_steps: int32 [64], P('blk'), may hold values from 1 to 9
- left_basis: float32 [64, 1024, 1024], P('blk', 'shard'), may hold values from -0.2 to 1.2, as said below
- right_basis: float32 [64, 1024, 1024], P('blk', 'shard'), may hold values from -0.2 to 1.2, as said below
- first_moment: float32 [64, 1024, 1024], P('blk', 'shard'), may hold values from -3 to 3
- second_moment: float32 [64, 1024, 1024], P('blk', 'shard'), may hold values from 0.016 to 1
Outputs:
- update: float32 [64, 1024, 1024], P(None, ('shard', 'blk'))
- new_first: float32 [64, 1024, 1024], P('blk', 'shard')
- new_second: float32 [64, 1024, 1024], P('blk', 'shard')
The draws below stay inside these ranges and needn't reach their ends.
Inputs may be any that keep to these rules, and one draw needn't show every extreme that they name: `owner_table`: each block number appears once. `left_basis`: nonsingular, not exactly orthogonal. `right_basis`: nonsingular, not exactly orthogonal.
All inputs are finite; a program needn't handle non-finite values.
Results may differ from the reference program's by a relative error of at most 0.0003.
Values sent between devices are 32-bit elements; how exact they have to be, the bound alone decides.
A program may use at most 64 MiB of HBM per device.

```python
import math
import jax
import jax.numpy as jnp
from jax import lax

ORDER = 1024
BLOCKS = 64


def draw_gradient(key, part):
    key = jax.random.fold_in(key, 11)
    keys = jax.random.split(key, 3)
    full_shape = (BLOCKS, ORDER, ORDER)
    row_scale = jnp.exp(jax.random.uniform(keys[0], (BLOCKS, ORDER, 1), jnp.float32, math.log(0.1), 0.0))
    col_scale = jnp.exp(jax.random.uniform(keys[1], (BLOCKS, 1, ORDER), jnp.float32, math.log(0.3), math.log(3.0)))
    rising = jnp.exp(0.5 * math.log(3.0) * jnp.arange(ORDER, dtype=jnp.float32) / (ORDER - 1)).reshape(1, ORDER, 1)
    values = jax.random.truncated_normal(keys[2], -4.0, 4.0, full_shape, jnp.float32)
    return values * row_scale * col_scale * rising


def identity_stack():
    positions = jnp.arange(ORDER, dtype=jnp.int32)
    return (positions[:, None] == positions[None, :]).astype(jnp.float32)[None, :, :]


def draw_left_basis(key, part):
    key = jax.random.fold_in(key, 21)
    noise = 0.5 * jax.random.truncated_normal(key, -4.0, 4.0, (BLOCKS, ORDER, ORDER), jnp.float32)
    return identity_stack() + noise / math.sqrt(ORDER)


def draw_right_basis(key, part):
    key = jax.random.fold_in(key, 22)
    noise = 0.5 * jax.random.truncated_normal(key, -4.0, 4.0, (BLOCKS, ORDER, ORDER), jnp.float32)
    return identity_stack() + noise / math.sqrt(ORDER)


def draw_second_moment(key, part):
    key = jax.random.fold_in(key, 31)
    values = jnp.exp(jax.random.uniform(key, (BLOCKS, ORDER, ORDER), jnp.float32, math.log(0.05), 0.0))
    falling = jnp.exp(-math.log(3.0) * jnp.arange(BLOCKS, dtype=jnp.float32) / (BLOCKS - 1)).reshape(BLOCKS, 1, 1)
    return values * falling


def touch_ends(array, key, least, high):
    spot = [jax.random.randint(jax.random.fold_in(key, axis), (), 0, length) for axis, length in enumerate(array.shape)]
    main_axis = array.shape.index(max(array.shape))
    beside = spot[:main_axis] + [(spot[main_axis] + 1) % array.shape[main_axis]] + spot[main_axis + 1:]
    return array.at[tuple(spot)].set(least).at[tuple(beside)].set(high)


def block_scale(rng, dims, cuts, low, top_value):
    def one(position, parts):
        heights = jax.random.uniform(jax.random.fold_in(jax.random.fold_in(rng, 6), position), (parts,), jnp.float32, low / len(cuts), top_value / len(cuts))
        return jnp.repeat(jnp.exp(heights), dims[position] // parts).reshape((-1,) + (1,) * (len(dims) - position - 1))

    loudness = one(*cuts[0])
    for cut in cuts[1:]:
        loudness = loudness * one(*cut)
    return loudness


def bell_draw(own_key, extent, width, limit, shards=(), kind=jnp.bfloat16):
    array = width * jax.random.normal(own_key, extent, jnp.float32)
    if shards:
        array = array * block_scale(own_key, extent, shards, -0.22, 0.18)
    return jnp.clip(array, -limit, limit).astype(kind)


def setup_inputs(seed: int = 0) -> dict:
    seeds = jax.random.split(jax.random.key(seed), 8)
    gradient = draw_gradient(jax.random.fold_in(seeds[7], 71), 0)
    owner_table = jax.random.permutation(seeds[1], BLOCKS).astype(jnp.int32)
    restart_steps = touch_ends(jax.random.randint(seeds[2], (BLOCKS,), 1, 10), jax.random.fold_in(seeds[2], 1), 1, 9).astype(jnp.int32)
    left_basis = draw_left_basis(jax.random.fold_in(seeds[7], 71), 0)
    right_basis = draw_right_basis(jax.random.fold_in(seeds[7], 71), 0)
    first_moment = bell_draw(seeds[5], (BLOCKS, ORDER, ORDER), 0.5, 3.0, ((0, 64), (1, 4)), jnp.float32)
    second_moment = draw_second_moment(jax.random.fold_in(seeds[7], 71), 0)
    return {"gradient": gradient, "owner_table": owner_table, "restart_steps": restart_steps, "left_basis": left_basis, "right_basis": right_basis, "first_moment": first_moment, "second_moment": second_moment}


BETA_ONE = 0.9
BETA_TWO = 0.95
EPSILON = 1e-08

def matmul(left_side, right_side):
    return jnp.dot(left_side, right_side, precision=lax.Precision.HIGHEST, preferred_element_type=jnp.float32)

def reference(gradient, owner_table, restart_steps, left_basis, right_basis, first_moment, second_moment):

    def rotate_slot(items):
        slot_block, step_count, left_tile, right_tile, first_old, second_old = items
        grad_block = lax.dynamic_index_in_dim(gradient, slot_block, 0, keepdims=False)
        rotated = matmul(matmul(left_tile.T, grad_block), right_tile)
        first_new = BETA_ONE * first_old + (1.0 - BETA_ONE) * rotated
        second_new = BETA_TWO * second_old + (1.0 - BETA_TWO) * rotated * rotated
        step_float = step_count.astype(jnp.float32)
        bias_first = 1.0 - jnp.power(jnp.float32(BETA_ONE), step_float)
        bias_second = 1.0 - jnp.power(jnp.float32(BETA_TWO), step_float)
        direction = first_new / bias_first / (jnp.sqrt(second_new / bias_second) + EPSILON)
        back_tile = matmul(matmul(left_tile, direction), right_tile.T)
        return (first_new, second_new, back_tile)
    new_first, new_second, back_all = lax.map(rotate_slot, (owner_table, restart_steps, left_basis, right_basis, first_moment, second_moment))
    grad_total = jnp.sum(gradient * gradient)
    back_total = jnp.sum(back_all * back_all)
    graft_scale = jnp.sqrt(grad_total / back_total)
    slot_ids = jnp.arange(owner_table.shape[0], dtype=jnp.int32)
    inverse = jnp.zeros_like(owner_table).at[owner_table].set(slot_ids)
    update = jnp.take(back_all, inverse, axis=0) * graft_scale
    return (update, new_first, new_second)
```

```python
import functools

import jax
import jax.numpy as jnp
from jax import lax
from jax.experimental import pallas as pl
from jax.experimental.pallas import tpu as pltpu
from jax.sharding import PartitionSpec as P

BETA_ONE = 0.9
BETA_TWO = 0.95
EPSILON = 1e-08
MESH = pl.DeviceIdType.MESH
F32 = jnp.float32
BF16 = jnp.bfloat16
NC = 4
W = 1024 // NC
Q = 256
NN = (((1,), (0,)), ((), ()))
NT = (((1,), (1,)), ((), ()))

SEMS = {}


def _sems(name, count=1):
    SEMS[name] = (sum(c for _, c in SEMS.values()), count)


for _name in ("L", "R", "M1", "M2", "RS", "RX", "RF", "BI", "G", "N1", "N2", "O", "SA", "SB"):
    _sems(_name)
for _name in ("A", "C", "X", "US", "UX", "UF"):
    _sems(_name, NC)
N_SEMS = sum(c for _, c in SEMS.values())


def split(value):
    high = value.astype(BF16)
    low = (value - high.astype(F32)).astype(BF16)
    return high, low


def dot3(ah, al, bh, bl, dims):
    dot = functools.partial(lax.dot_general, dimension_numbers=dims, preferred_element_type=F32)
    return dot(ah, bh) + (dot(ah, bl) + dot(al, bh))


def kernel(
    owner, inverse, grad, bias_in, left_in, right_in, first_in, second_in,
    update, first_out, second_out,
    send_g, recv_g, gh, gl, lf, lh, ll, lth, ltl, rf, rh, rl,
    a_snd, a_rcv, b_buf, c_snd, c_rcv, d_buf, x_rcv, rot, m1, m2, n1, n2, dh, dl,
    u_all, back, recv_o, bias, sa_v, sa_r, sb_v, sb_r, norm_g, norm_b, ssem, rsem, bar,
):
    b = lax.axis_index("blk")
    x = lax.axis_index("shard")
    y, z, c = b // 16, (b // 2) % 8, b % 2
    h = x // 2
    xp = x + 1 - 2 * (x % 2)
    home = c == h
    q = jnp.where(home, x, 3 - x)
    q_sib = 3 - q
    xp_q = xp + 0
    q_xp = jnp.where(home, xp_q, 3 - xp_q)
    q_xps = 3 - q_xp
    slot = (y * 8 + z) * 2 + h

    def dev(xx, yy, zz, cc):
        return {"shard": xx, "blk": (yy * 8 + zz) * 2 + cc}

    sib = dev(x, y, z, 1 - c)
    across = dev(xp, y, z, c)
    swap = dev(3 - x, y, z, 1 - c)

    def sem(ref, name, i=0):
        return ref.at[SEMS[name][0] + i]

    def rcopy(src, dst, name, to, i=0):
        return pltpu.make_async_remote_copy(
            src_ref=src, dst_ref=dst, send_sem=sem(ssem, name, i), recv_sem=sem(rsem, name, i),
            device_id=to, device_id_type=MESH,
        )

    def arrived(ref, name, i=0):
        pltpu.make_async_copy(ref, ref, sem(rsem, name, i)).wait()

    def sent(ref, name, i=0):
        pltpu.make_async_copy(ref, ref, sem(ssem, name, i)).wait()

    def zpeer(i):
        return dev(x, y, (z + i) % 8, c)

    def ypeer(i):
        return dev(x, (y + i) % 4, z, c)

    def xcpeer(i):
        xc = (x * 2 + c + i) % 8
        return dev(xc // 2, y, z, xc % 2)

    gate = pltpu.get_barrier_semaphore()
    for count, peer in ((8, zpeer), (4, ypeer), (8, xcpeer)):
        for i in range(1, count):
            pl.semaphore_signal(gate, inc=1, device_id=peer(i), device_id_type=MESH)
    pl.semaphore_wait(gate, 17)

    def fetch(src, dst, name):
        @pl.when(home)
        def _():
            pltpu.make_async_copy(src, dst, sem(rsem, name)).start()

        @pl.when(jnp.logical_not(home))
        def _():
            rcopy(src, dst, name, swap).start()

    rcopy(bias_in, bias, "BI", sib).start()

    @pl.when(home)
    def _():
        pltpu.make_async_copy(right_in.at[0], rf.at[q], sem(rsem, "R")).start()
        rcopy(right_in.at[0], rf.at[q], "RS", sib).start()
        rcopy(right_in.at[0], rf.at[q], "RX", across).start()

    @pl.when(jnp.logical_not(home))
    def _():
        rcopy(right_in.at[0], rf.at[x], "R", swap).start()

    fetch(left_in.at[0], lf, "L")

    norm_g[...] = jnp.zeros_like(norm_g)

    @pl.loop(0, 64)
    def _(o):
        send_g[o] = grad[owner[o]]
        mine = grad[o]
        square = mine * mine
        total = square[:, 0:128]
        for k in range(1, 8):
            total = total + square[:, k * 128:(k + 1) * 128]
        norm_g[...] += total

    for i in range(1, 4):
        pl.semaphore_signal(bar.at[0], inc=1, device_id=ypeer(i), device_id_type=MESH)
    pl.semaphore_wait(bar.at[0], 3)
    for i in range(1, 8):
        pl.semaphore_signal(bar.at[1], inc=1, device_id=xcpeer(i), device_id_type=MESH)
    pl.semaphore_wait(bar.at[1], 7)

    @pl.loop(0, 64)
    def _(t):
        yo, zo, co = (y + t // 16) % 4, (z + (t // 2) % 8) % 8, (c + t) % 2
        o = (yo * 8 + zo) * 2 + co
        xo = jnp.where(co == h, x, 3 - x)
        is_self = jnp.logical_and(home, t == 0)

        @pl.when(is_self)
        def _():
            pltpu.make_async_copy(send_g.at[o], recv_g.at[b], sem(rsem, "G")).start()

        @pl.when(jnp.logical_not(is_self))
        def _():
            rcopy(send_g.at[o], recv_g.at[b], "G", dev(xo, yo, zo, h)).start()

    def split_right(k):
        @pl.loop(0, 4)
        def _(i):
            rows = pl.ds(pl.multiple_of(i * 64, 64), 64)
            high, low = split(rf[k, rows, :])
            rh[k, rows, :] = high
            rl[k, rows, :] = low

    arrived(rf.at[q], "R")

    @pl.when(jnp.logical_not(home))
    def _():
        rcopy(rf.at[q], rf.at[q], "RS", sib).start()
        rcopy(rf.at[q], rf.at[q], "RX", across).start()

    split_right(q)
    arrived(rf.at[q_sib], "RS")
    split_right(q_sib)
    arrived(rf.at[q_xp], "RX")
    rcopy(rf.at[q_xp], rf.at[q_xp], "RF", sib).start()
    split_right(q_xp)
    arrived(rf.at[q_xps], "RF")
    split_right(q_xps)

    arrived(lf, "L")
    for k in range(4):
        cols = slice(k * Q, (k + 1) * Q)
        part = lf[:, cols]
        high, low = split(part)
        lh[:, cols] = high
        ll[:, cols] = low
        high, low = split(part.T)
        lth[k] = high
        ltl[k] = low

    arrived(recv_g, "G")

    @pl.loop(0, 16)
    def _(i):
        rows = pl.ds(pl.multiple_of(i * 16, 16), 16)
        part = jnp.concatenate([recv_g[i * 4 + k] for k in range(4)], axis=0)
        high, low = split(part)
        gh[rows, :] = high
        gl[rows, :] = low

    fetch(first_in.at[0], m1, "M1")
    fetch(second_in.at[0], m2, "M2")

    def partial(k, j):
        cols = slice(j * W, (j + 1) * W)
        return dot3(lth[k], ltl[k], gh[:, cols], gl[:, cols], NN)

    for j in range(NC):
        a_snd[j] = partial(q_xps, j)
        rcopy(a_snd.at[j], a_rcv.at[j], "A", sib, j).start()
    for j in range(NC):
        mine = partial(q_xp, j)
        arrived(a_rcv.at[j], "A", j)
        b_buf[j] = mine + a_rcv[j]
        rcopy(b_buf.at[j], x_rcv.at[j], "X", across, j).start()
    for j in range(NC):
        c_snd[j] = partial(q_sib, j)
        rcopy(c_snd.at[j], c_rcv.at[j], "C", sib, j).start()
    for j in range(NC):
        d_buf[j] = partial(q, j)

    for j in range(NC):
        arrived(c_rcv.at[j], "C", j)
        arrived(x_rcv.at[j], "X", j)
        th, tl = split(d_buf[j] + c_rcv[j] + x_rcv[j])
        per = Q // W if W < Q else 1
        rows = slice((j * W) % Q, (j * W) % Q + W)
        term = dot3(th, tl, rh[j * W // Q, rows, :], rl[j * W // Q, rows, :], NN)
        if j == 0:
            rot[...] = term
        else:
            rot[...] += term

    arrived(bias, "BI")
    arrived(m1, "M1")
    arrived(m2, "M2")
    biases = jnp.where(home, bias_in[...], bias[...])
    one_over = 1.0 / biases
    scale_one, scale_two = one_over[0:1, 0:1], one_over[1:2, 0:1]

    @pl.loop(0, 8)
    def _(i):
        rows = pl.ds(pl.multiple_of(i * 32, 32), 32)
        value = rot[rows, :]
        first_new = BETA_ONE * m1[rows, :] + (1.0 - BETA_ONE) * value
        second_new = BETA_TWO * m2[rows, :] + (1.0 - BETA_TWO) * value * value
        n1[rows, :] = first_new
        n2[rows, :] = second_new
        direction = (first_new * scale_one) / (jnp.sqrt(second_new * scale_two) + EPSILON)
        high, low = split(direction)
        dh[rows, :] = high
        dl[rows, :] = low

    for j in range(NC):
        rows = slice((j * W) % Q, (j * W) % Q + W)
        k = j * W // Q
        u_all[j, q] = dot3(dh[...], dl[...], rh[k, rows, :], rl[k, rows, :], NT)
        rcopy(u_all.at[j, q], u_all.at[j, q], "UX", across, j).start()
        rcopy(u_all.at[j, q], u_all.at[j, q], "US", sib, j).start()

    @pl.when(home)
    def _():
        pltpu.make_async_copy(n1, first_out.at[0], sem(rsem, "N1")).start()
        pltpu.make_async_copy(n2, second_out.at[0], sem(rsem, "N2")).start()

    @pl.when(jnp.logical_not(home))
    def _():
        rcopy(n1, first_out.at[0], "N1", swap).start()
        rcopy(n2, second_out.at[0], "N2", swap).start()

    norm_b[...] = jnp.zeros_like(norm_b)
    for j in range(NC):
        cols = slice(j * W, (j + 1) * W)
        arrived(u_all.at[j, q_xp], "UX", j)
        rcopy(u_all.at[j, q_xp], u_all.at[j, q_xp], "UF", sib, j).start()
        arrived(u_all.at[j, q_sib], "US", j)
        arrived(u_all.at[j, q_xps], "UF", j)
        uh, ul = split(u_all[j].reshape(1024, W))
        result = dot3(lh[...], ll[...], uh, ul, NN)
        square = result * result
        total = square[:, 0:128]
        for k in range(1, W // 128):
            total = total + square[:, k * 128:(k + 1) * 128]
        norm_b[...] += jnp.sum(total.reshape(32, 8, 128), axis=0)
        for i in range(64):
            back[i, :, cols] = result[i * 4:(i + 1) * 4, :]

        @pl.loop(0, 64)
        def _(t):
            yo, zo, co = (y + t // 16) % 4, (z + (t // 2) % 8) % 8, (c + t) % 2
            o = (yo * 8 + zo) * 2 + co
            is_self = jnp.logical_and(home, t == 0)

            @pl.when(is_self)
            def _():
                pltpu.make_async_copy(back.at[o, :, cols], recv_o.at[slot, :, cols], sem(rsem, "O")).start()

            @pl.when(jnp.logical_not(is_self))
            def _():
                rcopy(back.at[o, :, cols], recv_o.at[slot, :, cols], "O", dev(q, yo, zo, co)).start()

    sa_v[...] = jnp.concatenate(
        [norm_g[...], norm_b[0:4, :] + norm_b[4:8, :]], axis=0
    )
    zc = z * 2 + c

    @pl.loop(1, 16)
    def _(i):
        other = (zc + i) % 16
        rcopy(sa_v, sa_r.at[i - 1], "SA", dev(x, y, other // 2, other % 2)).start()

    arrived(sa_r, "SA")
    sb_v[...] = sa_v[...] + jnp.sum(sa_r[...], axis=0)
    xy = x * 4 + y

    @pl.loop(1, 16)
    def _(i):
        other = (xy + i) % 16
        rcopy(sb_v, sb_r.at[i - 1], "SB", dev(other // 4, other % 4, z, c)).start()

    arrived(sb_r, "SB")
    totals = sb_v[...] + jnp.sum(sb_r[...], axis=0)
    grad_total = jnp.sum(totals[0:4, :], keepdims=True)
    back_total = jnp.sum(totals[4:8, :], keepdims=True)
    graft = jnp.sqrt(grad_total / back_total)

    arrived(recv_o, "O")

    @pl.loop(0, 64)
    def _(k):
        update[k] = recv_o[inverse[k]] * graft

    sent(sa_r, "SA")
    sent(sb_r, "SB")
    sent(bias, "BI")
    sent(rf.at[0], "RS")
    sent(rf.at[0], "RX")
    sent(rf.at[0], "RF")
    for j in range(NC):
        sent(a_snd.at[j], "A", j)
        sent(b_buf.at[j], "X", j)
        sent(c_snd.at[j], "C", j)
        sent(u_all.at[0, 0], "US", j)
        sent(u_all.at[0, 0], "UX", j)
        sent(u_all.at[0, 0], "UF", j)
    arrived(n1, "N1")
    arrived(n2, "N2")

    @pl.when(home)
    def _():
        sent(recv_g.at[pl.ds(0, 63)], "G")
        sent(recv_o.at[pl.ds(0, 63)], "O")

    @pl.when(jnp.logical_not(home))
    def _():
        sent(recv_g, "G")
        sent(recv_o, "O")
        sent(lf, "L")
        sent(rf.at[0], "R")
        sent(m1, "M1")
        sent(m2, "M2")
        sent(n1, "N1")
        sent(n2, "N2")


def body(gradient, owner_table, restart_steps, left_basis, right_basis, first_moment, second_moment):
    slots = jnp.arange(64, dtype=jnp.int32)
    inverse = jnp.sum(
        jnp.where(owner_table[:, None] == slots[None, :], slots[:, None], 0), axis=0, dtype=jnp.int32
    )
    steps = restart_steps[0].astype(F32)
    bias_first = 1.0 - jnp.power(jnp.float32(BETA_ONE), steps)
    bias_second = 1.0 - jnp.power(jnp.float32(BETA_TWO), steps)
    row = lax.broadcasted_iota(jnp.int32, (8, 128), 0)
    bias = jnp.where(row == 0, bias_first, bias_second)

    vmem = pl.BlockSpec(memory_space=pltpu.VMEM)
    smem = pl.BlockSpec(memory_space=pltpu.SMEM)
    anywhere = pl.BlockSpec(memory_space=pl.ANY)
    rows_f = pltpu.VMEM((Q, 1024), F32)
    rows_b = pltpu.VMEM((Q, 1024), BF16)
    wire = pltpu.VMEM((64, 4, 1024), F32)
    chunks = pltpu.VMEM((NC, Q, W), F32)
    tile = pltpu.VMEM((8, 128), F32)
    lt = pltpu.VMEM((4, Q, Q), BF16)
    whole_b = pltpu.VMEM((4, Q, 1024), BF16)
    fifteen = pltpu.VMEM((15, 8, 128), F32)
    return pl.pallas_call(
        kernel,
        out_shape=(
            jax.ShapeDtypeStruct((64, 4, 1024), F32),
            jax.ShapeDtypeStruct((1, Q, 1024), F32),
            jax.ShapeDtypeStruct((1, Q, 1024), F32),
        ),
        in_specs=[smem, smem, vmem, vmem, anywhere, anywhere, anywhere, anywhere],
        out_specs=(vmem, anywhere, anywhere),
        scratch_shapes=[
            wire, wire, rows_b, rows_b, rows_f, rows_b, rows_b, lt, lt,
            pltpu.VMEM((4, Q, 1024), F32), whole_b, whole_b,
            chunks, chunks, chunks, chunks, chunks, chunks, chunks,
            rows_f, rows_f, rows_f, rows_f, rows_f, rows_b, rows_b,
            pltpu.VMEM((NC, 4, Q, W), F32), wire, wire,
            tile, tile, fifteen, tile, fifteen,
            pltpu.VMEM((4, 128), F32), tile,
            pltpu.SemaphoreType.DMA((N_SEMS,)),
            pltpu.SemaphoreType.DMA((N_SEMS,)),
            pltpu.SemaphoreType.REGULAR((2,)),
        ],
        compiler_params=pltpu.CompilerParams(
            collective_id=0, has_side_effects=True, vmem_limit_bytes=56 * 1024 * 1024
        ),
    )(owner_table, inverse, gradient, bias, left_basis, right_basis, first_moment, second_moment)


def solution(mesh):
    in_specs = (
        P(None, ("shard", "blk"), None),
        P(),
        P("blk"),
        P("blk", "shard", None),
        P("blk", "shard", None),
        P("blk", "shard", None),
        P("blk", "shard", None),
    )
    out_specs = (P(None, ("shard", "blk"), None), P("blk", "shard", None), P("blk", "shard", None))
    return jax.shard_map(body, mesh=mesh, in_specs=in_specs, out_specs=out_specs, check_vma=False)
```

```python
import functools

import jax
import jax.numpy as jnp
from jax import lax
from jax.experimental import pallas as pl
from jax.experimental.pallas import tpu as pltpu
from jax.sharding import PartitionSpec as P

BETA_ONE = 0.9
BETA_TWO = 0.95
EPSILON = 1e-08
MESH = pl.DeviceIdType.MESH
F32 = jnp.float32
BF16 = jnp.bfloat16
NC = 4
NG = 4
PER = NC // NG
CUTS = ((0, 128), (128, 128), (256, 256), (512, 256), (768, 256))
W = 1024 // NC
Q = 256
NN = (((1,), (0,)), ((), ()))
NT = (((1,), (1,)), ((), ()))

SEMS = {}


def _sems(name, count=1):
    SEMS[name] = (sum(c for _, c in SEMS.values()), count)


for _name in ("L", "R", "M1", "M2", "RS", "RX", "RF", "BI", "RO", "O", "SA", "SB", "GI"):
    _sems(_name)
_sems("G", NG)
for _name in ("A", "C", "X"):
    _sems(_name, NC)
for _name in ("US", "UX", "UF"):
    _sems(_name, len(CUTS))
N_SEMS = sum(c for _, c in SEMS.values())


def split(value):
    high = value.astype(BF16)
    low = (value - high.astype(F32)).astype(BF16)
    return high, low


def dot3(ah, al, bh, bl, dims):
    dot = functools.partial(lax.dot_general, dimension_numbers=dims, preferred_element_type=F32)
    return dot(ah, bh) + (dot(ah, bl) + dot(al, bh))


def kernel(
    owner, steps, grad_in, left_in, right_in, first_in, second_in,
    recv_o, rot_out, graft_out,
    grad, send_g, recv_g, gh, gl, lf, lh, ll, lth, ltl, rf, rh, rl,
    a_snd, a_rcv, b_buf, c_snd, c_rcv, d_buf, x_rcv, rot, m1, m2, dh, dl,
    u0, u1, u2, u3, u4, back, bias_mine, bias, sa_v, sa_r, sb_v, sb_r, norm_g, norm_b, ssem, rsem, bar,
):
    b = lax.axis_index("blk")
    x = lax.axis_index("shard")
    y, z, c = b // 16, (b // 2) % 8, b % 2
    h = x // 2
    xp = x + 1 - 2 * (x % 2)
    home = c == h
    u_all = (u0, u1, u2, u3, u4)
    away = c != h
    q = jnp.where(home, x, 3 - x)
    q_sib = 3 - q
    q_xp = jnp.where(home, xp, 3 - xp)
    q_xps = 3 - q_xp
    slot = (y * 8 + z) * 2 + h

    def dev(xx, yy, zz, cc):
        return {"shard": xx, "blk": (yy * 8 + zz) * 2 + cc}

    sib = dev(x, y, z, 1 - c)
    across = dev(xp, y, z, c)
    swap = dev(3 - x, y, z, 1 - c)

    def sem(ref, name, i=0):
        return ref.at[SEMS[name][0] + i]

    def rcopy(src, dst, name, to, i=0):
        return pltpu.make_async_remote_copy(
            src_ref=src, dst_ref=dst, send_sem=sem(ssem, name, i), recv_sem=sem(rsem, name, i),
            device_id=to, device_id_type=MESH,
        )

    def arrived(ref, name, i=0):
        pltpu.make_async_copy(ref, ref, sem(rsem, name, i)).wait()

    def sent(ref, name, i=0):
        pltpu.make_async_copy(ref, ref, sem(ssem, name, i)).wait()

    def zpeer(i):
        return dev(x, y, (z + i) % 8, c)

    def ypeer(i):
        return dev(x, (y + i) % 4, z, c)

    def xcpeer(i):
        xc = (x * 2 + c + i) % 8
        return dev(xc // 2, y, z, xc % 2)

    gate = pltpu.get_barrier_semaphore()
    for i in range(1, 8):
        pl.semaphore_signal(gate, inc=1, device_id=xcpeer(i), device_id_type=MESH)

    @pl.when(home)
    def _():
        for count, peer in ((8, zpeer), (4, ypeer)):
            for i in range(1, count):
                pl.semaphore_signal(gate, inc=1, device_id=peer(i), device_id_type=MESH)

    grad_copy = pltpu.make_async_copy(grad_in, grad, sem(rsem, "GI"))
    grad_copy.start()
    pl.semaphore_wait(gate, jnp.where(home, 17, 7))

    def fetch(src, dst, name):
        @pl.when(home)
        def _():
            pltpu.make_async_copy(src, dst, sem(rsem, name)).start()

        @pl.when(away)
        def _():
            rcopy(src, dst, name, swap).start()

    fetch(left_in.at[0], lf, "L")

    @pl.when(home)
    def _():
        rcopy(right_in.at[0], rf.at[q], "RX", across).start()
        rcopy(right_in.at[0], rf.at[q], "RS", sib).start()
        pltpu.make_async_copy(right_in.at[0], rf.at[q], sem(rsem, "R")).start()
        for i in range(1, 8):
            pl.semaphore_signal(bar.at[0], inc=1, device_id=zpeer(i), device_id_type=MESH)

    time = jnp.full((8, 128), steps[0].astype(F32))
    row = lax.broadcasted_iota(jnp.int32, (8, 128), 0)
    power = jnp.where(row == 0, jnp.power(jnp.float32(BETA_ONE), time), jnp.power(jnp.float32(BETA_TWO), time))
    bias_mine[...] = 1.0 - power
    rcopy(bias_mine, bias, "BI", sib).start()
    grad_copy.wait()

    @pl.loop(0, 64)
    def _(o):
        rows = grad[owner[o]]
        for k in range(NC):
            send_g[o, k] = rows[:, k * W:(k + 1) * W]

    @pl.when(home)
    def _():
        pl.semaphore_wait(bar.at[0], 7)
        for i in range(1, 4):
            pl.semaphore_signal(bar.at[1], inc=1, device_id=ypeer(i), device_id_type=MESH)
        pl.semaphore_wait(bar.at[1], 3)
        pl.semaphore_signal(bar.at[2], inc=1, device_id=sib, device_id_type=MESH)

    @pl.when(away)
    def _():
        pl.semaphore_wait(bar.at[2], 1)

    for g in range(NG):
        @pl.loop(0, 64)
        def _(t):
            yo, zo, co = (y + t // 16) % 4, (z + (t // 2) % 8) % 8, (c + t) % 2
            o = (yo * 8 + zo) * 2 + co
            xo = jnp.where(co == h, x, 3 - x)
            is_self = jnp.logical_and(home, t == 0)
            src = send_g.at[o, pl.ds((2 * co + g * PER) % NC, PER)]
            dst = recv_g.at[pl.ds(g * PER, PER), b]

            @pl.when(is_self)
            def _():
                pltpu.make_async_copy(src, dst, sem(rsem, "G", g)).start()

            @pl.when(jnp.logical_not(is_self))
            def _():
                rcopy(src, dst, "G", dev(xo, yo, zo, h), g).start()

        @pl.when(away)
        def _():
            part = pl.ds(g * (Q // NG), Q // NG)
            rcopy(right_in.at[0, part], rf.at[x, part], "R", swap).start()

    fetch(first_in.at[0], m1, "M1")
    fetch(second_in.at[0], m2, "M2")

    norm_g[...] = jnp.zeros_like(norm_g)

    @pl.loop(0, 64)
    def _(o):
        mine = grad[o]
        square = mine * mine
        total = square[:, 0:128]
        for k in range(1, 8):
            total = total + square[:, k * 128:(k + 1) * 128]
        norm_g[...] += total

    def split_right(k):
        @pl.loop(0, 4)
        def _(i):
            rows = pl.ds(pl.multiple_of(i * 64, 64), 64)
            high, low = split(rf[k, rows, :])
            rh[k, rows, :] = high
            rl[k, rows, :] = low

    @pl.when(home)
    def _():
        arrived(rf.at[q], "R")
        arrived(rf.at[q_xp], "RX")
        rcopy(rf.at[q_xp], rf.at[q_xp], "RF", sib).start()

    @pl.when(away)
    def _():
        arrived(rf.at[q_sib], "RS")
        arrived(rf.at[q_xps], "RF")

    split_right(2 * h)
    split_right(2 * h + 1)

    arrived(lf, "L")
    for k in range(4):
        cols = slice(k * Q, (k + 1) * Q)
        part = lf[:, cols]
        high, low = split(part)
        lh[:, cols] = high
        ll[:, cols] = low
        high, low = split(part.T)
        lth[k] = high
        ltl[k] = low

    def partial(k, i):
        return dot3(lth[k], ltl[k], gh[i], gl[i], NN)

    for i in range(NC):
        if i % PER == 0:
            arrived(recv_g.at[pl.ds(i, PER)], "G", i // PER)

        @pl.loop(0, 16)
        def _(k):
            rows = pl.ds(pl.multiple_of(k * 16, 16), 16)
            part = jnp.concatenate([recv_g[i, k * 4 + r] for r in range(4)], axis=0)
            high, low = split(part)
            gh[i, rows, :] = high
            gl[i, rows, :] = low

        a_snd[i] = partial(q_xps, i)
        rcopy(a_snd.at[i], a_rcv.at[i], "A", sib, i).start()
        mine = partial(q_xp, i)
        arrived(a_rcv.at[i], "A", i)
        b_buf[i] = mine + a_rcv[i]
        rcopy(b_buf.at[i], x_rcv.at[i], "X", across, i).start()
        c_snd[i] = partial(q_sib, i)
        rcopy(c_snd.at[i], c_rcv.at[i], "C", sib, i).start()
        d_buf[i] = partial(q, i)

    @pl.when(away)
    def _():
        arrived(rf.at[q], "R")
        rcopy(rf.at[q], rf.at[q], "RX", across).start()
        rcopy(rf.at[q], rf.at[q], "RS", sib).start()

    def rotate(i):
        arrived(c_rcv.at[i], "C", i)
        arrived(x_rcv.at[i], "X", i)
        k = (2 * h + i) % 4
        th, tl = split(d_buf[i] + c_rcv[i] + x_rcv[i])
        term = dot3(th, tl, rh[k], rl[k], NN)
        if i == 0:
            rot[...] = term
        else:
            rot[...] += term

    @pl.when(away)
    def _():
        arrived(rf.at[q_xp], "RX")
        rcopy(rf.at[q_xp], rf.at[q_xp], "RF", sib).start()

    @pl.when(home)
    def _():
        arrived(rf.at[q_sib], "RS")
        arrived(rf.at[q_xps], "RF")

    split_right(2 - 2 * h)
    split_right(3 - 2 * h)
    for i in range(NC):
        rotate(i)

    fetch_out = rot_out.at[0]

    @pl.when(home)
    def _():
        pltpu.make_async_copy(rot, fetch_out, sem(rsem, "RO")).start()

    @pl.when(away)
    def _():
        rcopy(rot, fetch_out, "RO", swap).start()

    arrived(bias, "BI")
    arrived(m1, "M1")
    arrived(m2, "M2")
    biases = jnp.where(home, bias_mine[...], bias[...])
    one_over = 1.0 / biases
    scale_one, scale_two = one_over[0:1, 0:1], one_over[1:2, 0:1]

    @pl.loop(0, 8)
    def _(i):
        rows = pl.ds(pl.multiple_of(i * 32, 32), 32)
        value = rot[rows, :]
        first_new = BETA_ONE * m1[rows, :] + (1.0 - BETA_ONE) * value
        second_new = BETA_TWO * m2[rows, :] + (1.0 - BETA_TWO) * value * value
        direction = (first_new * scale_one) / (jnp.sqrt(second_new * scale_two) + EPSILON)
        high, low = split(direction)
        dh[rows, :] = high
        dl[rows, :] = low

    for j, (start, width) in enumerate(CUTS):
        rows = slice(start % Q, start % Q + width)
        u_all[j][q] = dot3(dh[...], dl[...], rh[start // Q, rows, :], rl[start // Q, rows, :], NT)
        mine = u_all[j].at[q]
        rcopy(mine, mine, "UX", across, j).start()
        rcopy(mine, mine, "US", sib, j).start()

    norm_b[...] = jnp.zeros_like(norm_b)
    zc = z * 2 + c
    xy = x * 4 + y
    for j, (start, width) in enumerate(CUTS):
        cols = slice(start, start + width)
        theirs = u_all[j].at[q_xp]
        arrived(theirs, "UX", j)
        rcopy(theirs, theirs, "UF", sib, j).start()
        arrived(u_all[j].at[q_sib], "US", j)
        arrived(u_all[j].at[q_xps], "UF", j)
        uh, ul = split(u_all[j][...].reshape(1024, width))
        result = dot3(lh[...], ll[...], uh, ul, NN)
        square = result * result
        total = square[:, 0:128]
        for k in range(1, width // 128):
            total = total + square[:, k * 128:(k + 1) * 128]
        norm_b[...] += jnp.sum(total.reshape(32, 8, 128), axis=0)

        if j == len(CUTS) - 1:
            sa_v[...] = jnp.concatenate([norm_g[...], norm_b[0:4, :] + norm_b[4:8, :]], axis=0)

            @pl.loop(1, 16)
            def _(i):
                other = (zc + i) % 16
                rcopy(sa_v, sa_r.at[i - 1], "SA", dev(x, y, other // 2, other % 2)).start()

        for i in range(64):
            back[i, :, cols] = result[i * 4:(i + 1) * 4, :]

        @pl.loop(0, 64)
        def _(t):
            yo, zo, co = (y + t // 16) % 4, (z + (t // 2) % 8) % 8, (c + t) % 2
            o = (yo * 8 + zo) * 2 + co
            is_self = jnp.logical_and(home, t == 0)

            @pl.when(is_self)
            def _():
                pltpu.make_async_copy(back.at[o, :, cols], recv_o.at[slot, :, cols], sem(rsem, "O")).start()

            @pl.when(jnp.logical_not(is_self))
            def _():
                rcopy(back.at[o, :, cols], recv_o.at[slot, :, cols], "O", dev(q, yo, zo, co)).start()

    arrived(sa_r, "SA")
    sb_v[...] = sa_v[...] + jnp.sum(sa_r[...], axis=0)

    @pl.loop(1, 16)
    def _(i):
        other = (xy + i) % 16
        rcopy(sb_v, sb_r.at[i - 1], "SB", dev(other // 4, other % 4, z, c)).start()

    arrived(sb_r, "SB")
    totals = sb_v[...] + jnp.sum(sb_r[...], axis=0)
    grad_total = jnp.sum(totals[0:4, :], keepdims=True)
    back_total = jnp.sum(totals[4:8, :], keepdims=True)
    graft = jnp.sqrt(grad_total / back_total)
    graft_out[...] = jnp.broadcast_to(graft, (8, 128))
    arrived(recv_o, "O")
    arrived(rot, "RO")

    sent(sa_r, "SA")
    sent(sb_r, "SB")
    sent(bias, "BI")
    sent(rf.at[0], "RS")
    sent(rf.at[0], "RX")
    sent(rf.at[0], "RF")
    for j in range(NC):
        sent(a_snd.at[j], "A", j)
        sent(b_buf.at[j], "X", j)
        sent(c_snd.at[j], "C", j)
    for j in range(len(CUTS)):
        for name in ("US", "UX", "UF"):
            sent(u_all[j].at[0], name, j)

    @pl.when(home)
    def _():
        for g in range(NG):
            sent(recv_g.at[pl.ds(0, PER), pl.ds(0, 63)], "G", g)
        sent(recv_o.at[pl.ds(0, 63)], "O")

    @pl.when(away)
    def _():
        for g in range(NG):
            sent(recv_g.at[pl.ds(0, PER)], "G", g)
        sent(recv_o, "O")
        sent(lf, "L")
        sent(rf.at[0], "R")
        sent(m1, "M1")
        sent(m2, "M2")
        sent(rot, "RO")


def finish(
    owner, graft, received, rot_in, first_in, second_in, update, first_out, second_out,
    wire, rot, first, second, n1, n2, sin, sout,
):
    parts = 2
    size = Q // parts
    copy = pltpu.make_async_copy

    def pieces(p):
        rows = pl.ds(p * size, size)
        return [
            copy(src.at[0, rows], dst.at[rows], sin.at[p, k])
            for k, (src, dst) in enumerate(((rot_in, rot), (first_in, first), (second_in, second)))
        ]

    def results(p):
        rows = pl.ds(p * size, size)
        return [
            copy(src.at[rows], dst.at[0, rows], sout.at[p, k])
            for k, (src, dst) in enumerate(((n1, first_out), (n2, second_out)))
        ]

    incoming = copy(received, wire, sin.at[parts, 0])
    incoming.start()
    for p in range(parts):
        for piece in pieces(p):
            piece.start()
    scale = graft[0:1, 0:1]
    incoming.wait()

    @pl.loop(0, 64)
    def _(o):
        wire[o] = wire[o] * scale
        copy(wire.at[o], update.at[owner[o]], sout.at[parts, 0]).start()

    for p in range(parts):
        for piece in pieces(p):
            piece.wait()
        rows = pl.ds(p * size, size)
        value = rot[rows, :]
        n1[rows, :] = BETA_ONE * first[rows, :] + (1.0 - BETA_ONE) * value
        n2[rows, :] = BETA_TWO * second[rows, :] + (1.0 - BETA_TWO) * value * value
        for result in results(p):
            result.start()
    for p in range(parts):
        for result in results(p):
            result.wait()
    copy(wire, update, sout.at[parts, 0]).wait()


def body(gradient, owner_table, restart_steps, left_basis, right_basis, first_moment, second_moment):
    vmem = pl.BlockSpec(memory_space=pltpu.VMEM)
    smem = pl.BlockSpec(memory_space=pltpu.SMEM)
    anywhere = pl.BlockSpec(memory_space=pl.ANY)
    rows_f = pltpu.VMEM((Q, 1024), F32)
    rows_b = pltpu.VMEM((Q, 1024), BF16)
    wire = pltpu.VMEM((64, 4, 1024), F32)
    chunks = pltpu.VMEM((NC, Q, W), F32)
    chunks_b = pltpu.VMEM((NC, Q, W), BF16)
    tile = pltpu.VMEM((8, 128), F32)
    lt = pltpu.VMEM((4, Q, Q), BF16)
    whole_b = pltpu.VMEM((4, Q, 1024), BF16)
    fifteen = pltpu.VMEM((15, 8, 128), F32)
    received, rotated, graft = pl.pallas_call(
        kernel,
        out_shape=(
            jax.ShapeDtypeStruct((64, 4, 1024), F32),
            jax.ShapeDtypeStruct((1, Q, 1024), F32),
            jax.ShapeDtypeStruct((8, 128), F32),
        ),
        in_specs=[smem, smem, anywhere, anywhere, anywhere, anywhere, anywhere],
        out_specs=(anywhere, anywhere, vmem),
        scratch_shapes=[
            wire, pltpu.VMEM((64, NC, 4, W), F32), pltpu.VMEM((NC, 64, 4, W), F32),
            chunks_b, chunks_b, rows_f, rows_b, rows_b, lt, lt,
            pltpu.VMEM((4, Q, 1024), F32), whole_b, whole_b,
            chunks, chunks, chunks, chunks, chunks, chunks, chunks,
            rows_f, rows_f, rows_f, rows_b, rows_b,
            *(pltpu.VMEM((4, Q, width), F32) for _, width in CUTS), wire,
            tile, tile, tile, fifteen, tile, fifteen,
            pltpu.VMEM((4, 128), F32), tile,
            pltpu.SemaphoreType.DMA((N_SEMS,)),
            pltpu.SemaphoreType.DMA((N_SEMS,)),
            pltpu.SemaphoreType.REGULAR((3,)),
        ],
        compiler_params=pltpu.CompilerParams(
            collective_id=0, has_side_effects=True, vmem_limit_bytes=56 * 1024 * 1024
        ),
    )(owner_table, restart_steps, gradient, left_basis, right_basis, first_moment, second_moment)

    return pl.pallas_call(
        finish,
        out_shape=(
            jax.ShapeDtypeStruct((64, 4, 1024), F32),
            jax.ShapeDtypeStruct((1, Q, 1024), F32),
            jax.ShapeDtypeStruct((1, Q, 1024), F32),
        ),
        in_specs=[smem, vmem, anywhere, anywhere, anywhere, anywhere],
        out_specs=(anywhere, anywhere, anywhere),
        scratch_shapes=[
            wire, rows_f, rows_f, rows_f, rows_f, rows_f,
            pltpu.SemaphoreType.DMA((3, 3)), pltpu.SemaphoreType.DMA((3, 3)),
        ],
        compiler_params=pltpu.CompilerParams(vmem_limit_bytes=56 * 1024 * 1024),
    )(owner_table, graft, received, rotated, first_moment, second_moment)


def solution(mesh):
    in_specs = (
        P(None, ("shard", "blk"), None),
        P(),
        P("blk"),
        P("blk", "shard", None),
        P("blk", "shard", None),
        P("blk", "shard", None),
        P("blk", "shard", None),
    )
    out_specs = (P(None, ("shard", "blk"), None), P("blk", "shard", None), P("blk", "shard", None))
    return jax.shard_map(body, mesh=mesh, in_specs=in_specs, out_specs=out_specs, check_vma=False)
```

```python
import functools

import jax
import jax.numpy as jnp
from jax import lax
from jax.experimental import pallas as pl
from jax.experimental.pallas import tpu as pltpu
from jax.sharding import PartitionSpec as P

BETA_ONE = 0.9
BETA_TWO = 0.95
EPSILON = 1e-08
MESH = pl.DeviceIdType.MESH
F32 = jnp.float32
BF16 = jnp.bfloat16
NC = 4
NG = 2
PER = NC // NG
CUTS = ((0, 128), (128, 128), (256, 256), (512, 256), (768, 256))
W = 1024 // NC
Q = 256
NN = (((1,), (0,)), ((), ()))
NT = (((1,), (1,)), ((), ()))

SEMS = {}


def _sems(name, count=1):
    SEMS[name] = (sum(c for _, c in SEMS.values()), count)


for _name in ("L", "R", "M1", "M2", "RS", "RX", "RF", "BI", "RO", "O", "SA", "SB", "GI"):
    _sems(_name)
_sems("G", NG)
for _name in ("A", "C", "X"):
    _sems(_name, NC)
for _name in ("US", "UX", "UF"):
    _sems(_name, len(CUTS))
N_SEMS = sum(c for _, c in SEMS.values())


def split(value):
    high = value.astype(BF16)
    low = (value - high.astype(F32)).astype(BF16)
    return high, low


def dot3(ah, al, bh, bl, dims):
    dot = functools.partial(lax.dot_general, dimension_numbers=dims, preferred_element_type=F32)
    return dot(ah, bh) + (dot(ah, bl) + dot(al, bh))


def kernel(
    owner, steps, grad_in, left_in, right_in, first_in, second_in,
    recv_o, rot_out, graft_out,
    grad, send_g, recv_g, gh, gl, lf, lh, ll, lth, ltl, rf, rh, rl,
    a_snd, a_rcv, b_buf, c_snd, c_rcv, d_buf, x_rcv, rot, m1, m2, dh, dl,
    u0, u1, u2, u3, u4, back, bias_mine, bias, sa_v, sa_r, sb_v, sb_r, norm_g, norm_b, ssem, rsem, bar,
):
    b = lax.axis_index("blk")
    x = lax.axis_index("shard")
    y, z, c = b // 16, (b // 2) % 8, b % 2
    h = x // 2
    xp = x + 1 - 2 * (x % 2)
    home = c == h
    u_all = (u0, u1, u2, u3, u4)
    away = c != h
    q = jnp.where(home, x, 3 - x)
    q_sib = 3 - q
    q_xp = jnp.where(home, xp, 3 - xp)
    q_xps = 3 - q_xp
    slot = (y * 8 + z) * 2 + h

    def dev(xx, yy, zz, cc):
        return {"shard": xx, "blk": (yy * 8 + zz) * 2 + cc}

    sib = dev(x, y, z, 1 - c)
    across = dev(xp, y, z, c)
    swap = dev(3 - x, y, z, 1 - c)

    def sem(ref, name, i=0):
        return ref.at[SEMS[name][0] + i]

    def rcopy(src, dst, name, to, i=0):
        return pltpu.make_async_remote_copy(
            src_ref=src, dst_ref=dst, send_sem=sem(ssem, name, i), recv_sem=sem(rsem, name, i),
            device_id=to, device_id_type=MESH,
        )

    def arrived(ref, name, i=0):
        pltpu.make_async_copy(ref, ref, sem(rsem, name, i)).wait()

    def sent(ref, name, i=0):
        pltpu.make_async_copy(ref, ref, sem(ssem, name, i)).wait()

    def zpeer(i):
        return dev(x, y, (z + i) % 8, c)

    def ypeer(i):
        return dev(x, (y + i) % 4, z, c)

    def xcpeer(i):
        xc = (x * 2 + c + i) % 8
        return dev(xc // 2, y, z, xc % 2)

    gate = pltpu.get_barrier_semaphore()
    for i in range(1, 8):
        pl.semaphore_signal(gate, inc=1, device_id=xcpeer(i), device_id_type=MESH)

    @pl.when(home)
    def _():
        for count, peer in ((8, zpeer), (4, ypeer)):
            for i in range(1, count):
                pl.semaphore_signal(gate, inc=1, device_id=peer(i), device_id_type=MESH)

    grad_copy = pltpu.make_async_copy(grad_in, grad, sem(rsem, "GI"))
    grad_copy.start()
    pl.semaphore_wait(gate, jnp.where(home, 17, 7))

    def fetch(src, dst, name):
        @pl.when(home)
        def _():
            pltpu.make_async_copy(src, dst, sem(rsem, name)).start()

        @pl.when(away)
        def _():
            rcopy(src, dst, name, swap).start()

    @pl.when(home)
    def _():
        rcopy(right_in.at[0], rf.at[q], "RX", across).start()
        rcopy(right_in.at[0], rf.at[q], "RS", sib).start()
        pltpu.make_async_copy(right_in.at[0], rf.at[q], sem(rsem, "R")).start()
        for i in range(1, 8):
            pl.semaphore_signal(bar.at[0], inc=1, device_id=zpeer(i), device_id_type=MESH)

    @pl.when(away)
    def _():
        rcopy(right_in.at[0], rf.at[x], "R", swap).start()

    time = jnp.full((8, 128), steps[0].astype(F32))
    row = lax.broadcasted_iota(jnp.int32, (8, 128), 0)
    power = jnp.where(row == 0, jnp.power(jnp.float32(BETA_ONE), time), jnp.power(jnp.float32(BETA_TWO), time))
    bias_mine[...] = 1.0 - power
    rcopy(bias_mine, bias, "BI", sib).start()
    grad_copy.wait()

    @pl.loop(0, 64)
    def _(o):
        rows = grad[owner[o]]
        for k in range(NC):
            send_g[o, k] = rows[:, k * W:(k + 1) * W]

    @pl.when(home)
    def _():
        pl.semaphore_wait(bar.at[0], 7)
        for i in range(1, 4):
            pl.semaphore_signal(bar.at[1], inc=1, device_id=ypeer(i), device_id_type=MESH)
        pl.semaphore_wait(bar.at[1], 3)
        pl.semaphore_signal(bar.at[2], inc=1, device_id=sib, device_id_type=MESH)

    @pl.when(away)
    def _():
        pl.semaphore_wait(bar.at[2], 1)

    for g in range(NG):
        part = pl.ds(g * (Q // NG), Q // NG)
        fetch(left_in.at[0, part], lf.at[part], "L")

        @pl.loop(0, 64)
        def _(t):
            yo, zo, co = (y + t // 16) % 4, (z + 3 * (t // 2)) % 8, (c + t) % 2
            o = (yo * 8 + zo) * 2 + co
            xo = jnp.where(co == h, x, 3 - x)
            is_self = jnp.logical_and(home, t == 0)
            src = send_g.at[o, pl.ds((2 * co + g * PER) % NC, PER)]
            dst = recv_g.at[pl.ds(g * PER, PER), b]

            @pl.when(is_self)
            def _():
                pltpu.make_async_copy(src, dst, sem(rsem, "G", g)).start()

            @pl.when(jnp.logical_not(is_self))
            def _():
                rcopy(src, dst, "G", dev(xo, yo, zo, h), g).start()

    fetch(first_in.at[0], m1, "M1")
    fetch(second_in.at[0], m2, "M2")

    norm_g[...] = jnp.zeros_like(norm_g)

    @pl.loop(0, 64)
    def _(o):
        mine = grad[o]
        square = mine * mine
        total = square[:, 0:128]
        for k in range(1, 8):
            total = total + square[:, k * 128:(k + 1) * 128]
        norm_g[...] += total

    def split_right(k):
        @pl.loop(0, 4)
        def _(i):
            rows = pl.ds(pl.multiple_of(i * 64, 64), 64)
            high, low = split(rf[k, rows, :])
            rh[k, rows, :] = high
            rl[k, rows, :] = low

    @pl.when(away)
    def _():
        arrived(rf.at[q], "R")
        rcopy(rf.at[q], rf.at[q], "RX", across).start()
        rcopy(rf.at[q], rf.at[q], "RS", sib).start()

    @pl.when(home)
    def _():
        arrived(rf.at[q], "R")
        arrived(rf.at[q_xp], "RX")
        rcopy(rf.at[q_xp], rf.at[q_xp], "RF", sib).start()
        arrived(rf.at[q_sib], "RS")

    @pl.when(away)
    def _():
        arrived(rf.at[q_sib], "RS")
        arrived(rf.at[q_xps], "RF")

    split_right(q)
    split_right(q_sib)

    @pl.when(away)
    def _():
        arrived(rf.at[q_xp], "RX")
        rcopy(rf.at[q_xp], rf.at[q_xp], "RF", sib).start()

    @pl.when(home)
    def _():
        arrived(rf.at[q_xps], "RF")

    split_right(q_xp)
    split_right(q_xps)

    arrived(lf, "L")
    for k in range(4):
        cols = slice(k * Q, (k + 1) * Q)
        part = lf[:, cols]
        high, low = split(part)
        lh[:, cols] = high
        ll[:, cols] = low
        high, low = split(part.T)
        lth[k] = high
        ltl[k] = low

    def partial(k, i):
        return dot3(lth[k], ltl[k], gh[i], gl[i], NN)

    for i in range(NC):
        if i % PER == 0:
            arrived(recv_g.at[pl.ds(i, PER)], "G", i // PER)

        @pl.loop(0, 16)
        def _(k):
            rows = pl.ds(pl.multiple_of(k * 16, 16), 16)
            part = jnp.concatenate([recv_g[i, k * 4 + r] for r in range(4)], axis=0)
            high, low = split(part)
            gh[i, rows, :] = high
            gl[i, rows, :] = low

        a_snd[i] = partial(q_xps, i)
        rcopy(a_snd.at[i], a_rcv.at[i], "A", sib, i).start()
        mine = partial(q_xp, i)
        arrived(a_rcv.at[i], "A", i)
        b_buf[i] = mine + a_rcv[i]
        rcopy(b_buf.at[i], x_rcv.at[i], "X", across, i).start()
        c_snd[i] = partial(q_sib, i)
        rcopy(c_snd.at[i], c_rcv.at[i], "C", sib, i).start()
        d_buf[i] = partial(q, i)

    for i in range(NC):
        arrived(c_rcv.at[i], "C", i)
        arrived(x_rcv.at[i], "X", i)
        k = (2 * h + i) % 4
        th, tl = split(d_buf[i] + c_rcv[i] + x_rcv[i])
        term = dot3(th, tl, rh[k], rl[k], NN)
        if i == 0:
            rot[...] = term
        else:
            rot[...] += term

    arrived(bias, "BI")
    arrived(m1, "M1")
    arrived(m2, "M2")
    biases = jnp.where(home, bias_mine[...], bias[...])
    one_over = 1.0 / biases
    scale_one, scale_two = one_over[0:1, 0:1], one_over[1:2, 0:1]

    @pl.loop(0, 8)
    def _(i):
        rows = pl.ds(pl.multiple_of(i * 32, 32), 32)
        value = rot[rows, :]
        first_new = BETA_ONE * m1[rows, :] + (1.0 - BETA_ONE) * value
        second_new = BETA_TWO * m2[rows, :] + (1.0 - BETA_TWO) * value * value
        direction = (first_new * scale_one) / (jnp.sqrt(second_new * scale_two) + EPSILON)
        high, low = split(direction)
        dh[rows, :] = high
        dl[rows, :] = low

    for j, (start, width) in enumerate(CUTS):
        rows = slice(start % Q, start % Q + width)
        u_all[j][q] = dot3(dh[...], dl[...], rh[start // Q, rows, :], rl[start // Q, rows, :], NT)
        mine = u_all[j].at[q]
        rcopy(mine, mine, "UX", across, j).start()
        rcopy(mine, mine, "US", sib, j).start()

    norm_b[...] = jnp.zeros_like(norm_b)
    zc = z * 2 + c
    xy = x * 4 + y
    for j, (start, width) in enumerate(CUTS):
        cols = slice(start, start + width)
        theirs = u_all[j].at[q_xp]
        arrived(theirs, "UX", j)
        rcopy(theirs, theirs, "UF", sib, j).start()
        arrived(u_all[j].at[q_sib], "US", j)
        arrived(u_all[j].at[q_xps], "UF", j)
        uh, ul = split(u_all[j][...].reshape(1024, width))
        result = dot3(lh[...], ll[...], uh, ul, NN)
        square = result * result
        total = square[:, 0:128]
        for k in range(1, width // 128):
            total = total + square[:, k * 128:(k + 1) * 128]
        norm_b[...] += jnp.sum(total.reshape(32, 8, 128), axis=0)

        if j == len(CUTS) - 1:
            sa_v[...] = jnp.concatenate([norm_g[...], norm_b[0:4, :] + norm_b[4:8, :]], axis=0)

            @pl.loop(1, 16)
            def _(i):
                other = (zc + i) % 16
                rcopy(sa_v, sa_r.at[i - 1], "SA", dev(x, y, other // 2, other % 2)).start()

        for i in range(64):
            back[i, :, cols] = result[i * 4:(i + 1) * 4, :]

        @pl.loop(0, 64)
        def _(t):
            yo, zo, co = (y + t // 16) % 4, (z + 3 * (t // 2)) % 8, (c + t) % 2
            o = (yo * 8 + zo) * 2 + co
            is_self = jnp.logical_and(home, t == 0)

            @pl.when(is_self)
            def _():
                pltpu.make_async_copy(back.at[o, :, cols], recv_o.at[slot, :, cols], sem(rsem, "O")).start()

            @pl.when(jnp.logical_not(is_self))
            def _():
                rcopy(back.at[o, :, cols], recv_o.at[slot, :, cols], "O", dev(q, yo, zo, co)).start()

        if 1 <= j <= 2:
            part = pl.ds((j - 1) * 128, 128)
            fetch(rot.at[part], rot_out.at[0, part], "RO")

    arrived(sa_r, "SA")
    sb_v[...] = sa_v[...] + jnp.sum(sa_r[...], axis=0)

    @pl.loop(1, 16)
    def _(i):
        other = (xy + i) % 16
        rcopy(sb_v, sb_r.at[i - 1], "SB", dev(other // 4, other % 4, z, c)).start()

    arrived(sb_r, "SB")
    totals = sb_v[...] + jnp.sum(sb_r[...], axis=0)
    grad_total = jnp.sum(totals[0:4, :], keepdims=True)
    back_total = jnp.sum(totals[4:8, :], keepdims=True)
    graft = jnp.sqrt(grad_total / back_total)
    graft_out[...] = jnp.broadcast_to(graft, (8, 128))
    arrived(recv_o, "O")
    arrived(rot, "RO")

    sent(sa_r, "SA")
    sent(sb_r, "SB")
    sent(bias, "BI")
    sent(rf.at[0], "RS")
    sent(rf.at[0], "RX")
    sent(rf.at[0], "RF")
    for j in range(NC):
        sent(a_snd.at[j], "A", j)
        sent(b_buf.at[j], "X", j)
        sent(c_snd.at[j], "C", j)
    for j in range(len(CUTS)):
        for name in ("US", "UX", "UF"):
            sent(u_all[j].at[0], name, j)

    @pl.when(home)
    def _():
        for g in range(NG):
            sent(recv_g.at[pl.ds(0, PER), pl.ds(0, 63)], "G", g)
        sent(recv_o.at[pl.ds(0, 63)], "O")

    @pl.when(away)
    def _():
        for g in range(NG):
            sent(recv_g.at[pl.ds(0, PER)], "G", g)
        sent(recv_o, "O")
        sent(lf, "L")
        sent(rf.at[0], "R")
        sent(m1, "M1")
        sent(m2, "M2")
        sent(rot, "RO")


def finish(
    owner, graft, received, rot_in, first_in, second_in, update, first_out, second_out,
    wire, rot, first, second, n1, n2, sin, sout,
):
    parts = 4
    size = Q // parts
    slots = 64 // parts
    copy = pltpu.make_async_copy

    def pieces(p):
        rows = pl.ds(p * size, size)
        return [
            copy(src.at[0, rows], dst.at[rows], sin.at[p, k])
            for k, (src, dst) in enumerate(((rot_in, rot), (first_in, first), (second_in, second)))
        ]

    def results(p):
        rows = pl.ds(p * size, size)
        return [
            copy(src.at[rows], dst.at[0, rows], sout.at[p, k])
            for k, (src, dst) in enumerate(((n1, first_out), (n2, second_out)))
        ]

    def incoming(p):
        some = pl.ds(p * slots, slots)
        return copy(received.at[some], wire.at[some], sin.at[p, 3])

    for p in range(parts):
        for piece in pieces(p):
            piece.start()
    for p in range(parts):
        incoming(p).start()
    for p in range(parts):
        for piece in pieces(p):
            piece.wait()
        rows = pl.ds(p * size, size)
        value = rot[rows, :]
        n1[rows, :] = BETA_ONE * first[rows, :] + (1.0 - BETA_ONE) * value
        n2[rows, :] = BETA_TWO * second[rows, :] + (1.0 - BETA_TWO) * value * value
        for result in results(p):
            result.start()
    scale = graft[0:1, 0:1]
    for p in range(parts):
        incoming(p).wait()

        @pl.loop(0, slots, unroll=4)
        def _(i):
            o = p * slots + i
            wire[o] = wire[o] * scale
            copy(wire.at[o], update.at[owner[o]], sout.at[parts, 0]).start()

    for p in range(parts):
        for result in results(p):
            result.wait()
    copy(wire, update, sout.at[parts, 0]).wait()


def body(gradient, owner_table, restart_steps, left_basis, right_basis, first_moment, second_moment):
    vmem = pl.BlockSpec(memory_space=pltpu.VMEM)
    smem = pl.BlockSpec(memory_space=pltpu.SMEM)
    anywhere = pl.BlockSpec(memory_space=pl.ANY)
    rows_f = pltpu.VMEM((Q, 1024), F32)
    rows_b = pltpu.VMEM((Q, 1024), BF16)
    wire = pltpu.VMEM((64, 4, 1024), F32)
    chunks = pltpu.VMEM((NC, Q, W), F32)
    chunks_b = pltpu.VMEM((NC, Q, W), BF16)
    tile = pltpu.VMEM((8, 128), F32)
    lt = pltpu.VMEM((4, Q, Q), BF16)
    whole_b = pltpu.VMEM((4, Q, 1024), BF16)
    fifteen = pltpu.VMEM((15, 8, 128), F32)
    received, rotated, graft = pl.pallas_call(
        kernel,
        out_shape=(
            jax.ShapeDtypeStruct((64, 4, 1024), F32),
            jax.ShapeDtypeStruct((1, Q, 1024), F32),
            jax.ShapeDtypeStruct((8, 128), F32),
        ),
        in_specs=[smem, smem, anywhere, anywhere, anywhere, anywhere, anywhere],
        out_specs=(anywhere, anywhere, vmem),
        scratch_shapes=[
            wire, pltpu.VMEM((64, NC, 4, W), F32), pltpu.VMEM((NC, 64, 4, W), F32),
            chunks_b, chunks_b, rows_f, rows_b, rows_b, lt, lt,
            pltpu.VMEM((4, Q, 1024), F32), whole_b, whole_b,
            chunks, chunks, chunks, chunks, chunks, chunks, chunks,
            rows_f, rows_f, rows_f, rows_b, rows_b,
            *(pltpu.VMEM((4, Q, width), F32) for _, width in CUTS), wire,
            tile, tile, tile, fifteen, tile, fifteen,
            pltpu.VMEM((4, 128), F32), tile,
            pltpu.SemaphoreType.DMA((N_SEMS,)),
            pltpu.SemaphoreType.DMA((N_SEMS,)),
            pltpu.SemaphoreType.REGULAR((3,)),
        ],
        compiler_params=pltpu.CompilerParams(
            collective_id=0, has_side_effects=True, vmem_limit_bytes=56 * 1024 * 1024
        ),
    )(owner_table, restart_steps, gradient, left_basis, right_basis, first_moment, second_moment)

    return pl.pallas_call(
        finish,
        out_shape=(
            jax.ShapeDtypeStruct((64, 4, 1024), F32),
            jax.ShapeDtypeStruct((1, Q, 1024), F32),
            jax.ShapeDtypeStruct((1, Q, 1024), F32),
        ),
        in_specs=[smem, vmem, anywhere, anywhere, anywhere, anywhere],
        out_specs=(anywhere, anywhere, anywhere),
        scratch_shapes=[
            wire, rows_f, rows_f, rows_f, rows_f, rows_f,
            pltpu.SemaphoreType.DMA((4, 4)), pltpu.SemaphoreType.DMA((5, 2)),
        ],
        compiler_params=pltpu.CompilerParams(vmem_limit_bytes=56 * 1024 * 1024),
    )(owner_table, graft, received, rotated, first_moment, second_moment)


def solution(mesh):
    in_specs = (
        P(None, ("shard", "blk"), None),
        P(),
        P("blk"),
        P("blk", "shard", None),
        P("blk", "shard", None),
        P("blk", "shard", None),
        P("blk", "shard", None),
    )
    out_specs = (P(None, ("shard", "blk"), None), P("blk", "shard", None), P("blk", "shard", None))
    return jax.shard_map(body, mesh=mesh, in_specs=in_specs, out_specs=out_specs, check_vma=False)
```

```python
import functools

import jax
import jax.numpy as jnp
from jax import lax
from jax.experimental import pallas as pl
from jax.experimental.pallas import tpu as pltpu
from jax.sharding import PartitionSpec as P

BETA_ONE = 0.9
BETA_TWO = 0.95
EPSILON = 1e-08
MESH = pl.DeviceIdType.MESH
F32 = jnp.float32
BF16 = jnp.bfloat16
NC = 4
NG = 2
PER = NC // NG
CUTS = ((0, 128), (128, 128), (256, 256), (512, 256), (768, 256))
W = 1024 // NC
Q = 256
NN = (((1,), (0,)), ((), ()))
NT = (((1,), (1,)), ((), ()))

SEMS = {}


def _sems(name, count=1):
    SEMS[name] = (sum(c for _, c in SEMS.values()), count)


for _name in ("L", "R", "M1", "M2", "RS", "RX", "RF", "BI", "RO", "O", "SA", "SB", "GI"):
    _sems(_name)
_sems("G", NG)
for _name in ("A", "C", "X"):
    _sems(_name, NC)
for _name in ("US", "UX", "UF"):
    _sems(_name, len(CUTS))
N_SEMS = sum(c for _, c in SEMS.values())


def split(value):
    high = value.astype(BF16)
    low = (value - high.astype(F32)).astype(BF16)
    return high, low


def dot3(ah, al, bh, bl, dims):
    dot = functools.partial(lax.dot_general, dimension_numbers=dims, preferred_element_type=F32)
    return dot(ah, bh) + (dot(ah, bl) + dot(al, bh))


def kernel(
    owner, steps, grad_in, left_in, right_in, first_in, second_in,
    recv_o, rot_out, graft_out,
    grad, send_g, recv_g, gh, gl, lf, lh, ll, lth, ltl, rf, rh, rl,
    a_snd, a_rcv, b_buf, c_snd, c_rcv, d_buf, x_rcv, rot, m1, m2, dh, dl,
    u0, u1, u2, u3, u4, back, bias_mine, bias, sa_v, sa_r, sb_v, sb_r, norm_g, norm_b, ssem, rsem, bar,
):
    b = lax.axis_index("blk")
    x = lax.axis_index("shard")
    y, z, c = b // 16, (b // 2) % 8, b % 2
    h = x // 2
    xp = x + 1 - 2 * (x % 2)
    home = c == h
    u_all = (u0, u1, u2, u3, u4)
    away = c != h
    q = jnp.where(home, x, 3 - x)
    q_sib = 3 - q
    q_xp = jnp.where(home, xp, 3 - xp)
    q_xps = 3 - q_xp
    slot = (y * 8 + z) * 2 + h

    def dev(xx, yy, zz, cc):
        return {"shard": xx, "blk": (yy * 8 + zz) * 2 + cc}

    sib = dev(x, y, z, 1 - c)
    across = dev(xp, y, z, c)
    swap = dev(3 - x, y, z, 1 - c)

    def sem(ref, name, i=0):
        return ref.at[SEMS[name][0] + i]

    def rcopy(src, dst, name, to, i=0):
        return pltpu.make_async_remote_copy(
            src_ref=src, dst_ref=dst, send_sem=sem(ssem, name, i), recv_sem=sem(rsem, name, i),
            device_id=to, device_id_type=MESH,
        )

    def arrived(ref, name, i=0):
        pltpu.make_async_copy(ref, ref, sem(rsem, name, i)).wait()

    def sent(ref, name, i=0):
        pltpu.make_async_copy(ref, ref, sem(ssem, name, i)).wait()

    def zpeer(i):
        return dev(x, y, (z + i) % 8, c)

    def ypeer(i):
        return dev(x, (y + i) % 4, z, c)

    def xcpeer(i):
        xc = (x * 2 + c + i) % 8
        return dev(xc // 2, y, z, xc % 2)

    gate = pltpu.get_barrier_semaphore()
    @pl.when(home)
    def _():
        for count, peer in ((8, zpeer), (4, ypeer)):
            for i in range(1, count):
                pl.semaphore_signal(gate, inc=1, device_id=peer(i), device_id_type=MESH)

    for i in range(1, 8):
        pl.semaphore_signal(gate, inc=1, device_id=xcpeer(i), device_id_type=MESH)

    grad_copy = pltpu.make_async_copy(grad_in, grad, sem(rsem, "GI"))
    grad_copy.start()
    pl.semaphore_wait(gate, jnp.where(home, 17, 7))

    def fetch(src, dst, name):
        @pl.when(home)
        def _():
            pltpu.make_async_copy(src, dst, sem(rsem, name)).start()

        @pl.when(away)
        def _():
            rcopy(src, dst, name, swap).start()

    @pl.when(home)
    def _():
        rcopy(right_in.at[0], rf.at[q], "RX", across).start()
        rcopy(right_in.at[0], rf.at[q], "RS", sib).start()
        pltpu.make_async_copy(right_in.at[0], rf.at[q], sem(rsem, "R")).start()
        for i in range(1, 8):
            pl.semaphore_signal(bar.at[0], inc=1, device_id=zpeer(i), device_id_type=MESH)

    @pl.when(away)
    def _():
        rcopy(right_in.at[0], rf.at[x], "R", swap).start()

    time = jnp.full((8, 128), steps[0].astype(F32))
    row = lax.broadcasted_iota(jnp.int32, (8, 128), 0)
    power = jnp.where(row == 0, jnp.power(jnp.float32(BETA_ONE), time), jnp.power(jnp.float32(BETA_TWO), time))
    bias_mine[...] = 1.0 - power
    rcopy(bias_mine, bias, "BI", sib).start()
    grad_copy.wait()

    @pl.loop(0, 64)
    def _(o):
        rows = grad[owner[o]]
        for k in range(NC):
            send_g[o, k] = rows[:, k * W:(k + 1) * W]

    @pl.when(home)
    def _():
        pl.semaphore_wait(bar.at[0], 7)
        for i in range(1, 4):
            pl.semaphore_signal(bar.at[1], inc=1, device_id=ypeer(i), device_id_type=MESH)
        pl.semaphore_wait(bar.at[1], 3)
        pl.semaphore_signal(bar.at[2], inc=1, device_id=sib, device_id_type=MESH)

    @pl.when(away)
    def _():
        pl.semaphore_wait(bar.at[2], 1)

    for g in range(NG):
        part = pl.ds(g * (Q // NG), Q // NG)
        fetch(left_in.at[0, part], lf.at[part], "L")

        @pl.loop(0, 64)
        def _(t):
            yo, zo, co = (y + t // 16) % 4, (z + 3 * (t // 2)) % 8, (c + t) % 2
            o = (yo * 8 + zo) * 2 + co
            xo = jnp.where(co == h, x, 3 - x)
            is_self = jnp.logical_and(home, t == 0)
            src = send_g.at[o, pl.ds((2 * co + g * PER) % NC, PER)]
            dst = recv_g.at[pl.ds(g * PER, PER), b]

            @pl.when(is_self)
            def _():
                pltpu.make_async_copy(src, dst, sem(rsem, "G", g)).start()

            @pl.when(jnp.logical_not(is_self))
            def _():
                rcopy(src, dst, "G", dev(xo, yo, zo, h), g).start()

    fetch(first_in.at[0], m1, "M1")
    fetch(second_in.at[0], m2, "M2")

    norm_g[...] = jnp.zeros_like(norm_g)

    @pl.loop(0, 64)
    def _(o):
        mine = grad[o]
        square = mine * mine
        total = square[:, 0:128]
        for k in range(1, 8):
            total = total + square[:, k * 128:(k + 1) * 128]
        norm_g[...] += total

    def split_right(k):
        @pl.loop(0, 4)
        def _(i):
            rows = pl.ds(pl.multiple_of(i * 64, 64), 64)
            high, low = split(rf[k, rows, :])
            rh[k, rows, :] = high
            rl[k, rows, :] = low

    @pl.when(away)
    def _():
        arrived(rf.at[q], "R")
        rcopy(rf.at[q], rf.at[q], "RX", across).start()
        rcopy(rf.at[q], rf.at[q], "RS", sib).start()

    @pl.when(home)
    def _():
        arrived(rf.at[q], "R")
        arrived(rf.at[q_xp], "RX")
        rcopy(rf.at[q_xp], rf.at[q_xp], "RF", sib).start()
        arrived(rf.at[q_sib], "RS")

    @pl.when(away)
    def _():
        arrived(rf.at[q_sib], "RS")
        arrived(rf.at[q_xps], "RF")

    split_right(q)
    split_right(q_sib)

    @pl.when(away)
    def _():
        arrived(rf.at[q_xp], "RX")
        rcopy(rf.at[q_xp], rf.at[q_xp], "RF", sib).start()

    @pl.when(home)
    def _():
        arrived(rf.at[q_xps], "RF")

    split_right(q_xp)
    split_right(q_xps)

    arrived(lf, "L")
    for k in range(4):
        cols = slice(k * Q, (k + 1) * Q)
        part = lf[:, cols]
        high, low = split(part)
        lh[:, cols] = high
        ll[:, cols] = low
        high, low = split(part.T)
        lth[k] = high
        ltl[k] = low

    def partial(k, i):
        return dot3(lth[k], ltl[k], gh[i], gl[i], NN)

    for i in range(NC):
        if i % PER == 0:
            arrived(recv_g.at[pl.ds(i, PER)], "G", i // PER)

        @pl.loop(0, 16)
        def _(k):
            rows = pl.ds(pl.multiple_of(k * 16, 16), 16)
            part = jnp.concatenate([recv_g[i, k * 4 + r] for r in range(4)], axis=0)
            high, low = split(part)
            gh[i, rows, :] = high
            gl[i, rows, :] = low

        a_snd[i] = partial(q_xps, i)
        rcopy(a_snd.at[i], a_rcv.at[i], "A", sib, i).start()
        mine = partial(q_xp, i)
        arrived(a_rcv.at[i], "A", i)
        b_buf[i] = mine + a_rcv[i]
        rcopy(b_buf.at[i], x_rcv.at[i], "X", across, i).start()
        c_snd[i] = partial(q_sib, i)
        rcopy(c_snd.at[i], c_rcv.at[i], "C", sib, i).start()
        d_buf[i] = partial(q, i)

    for i in range(NC):
        arrived(c_rcv.at[i], "C", i)
        arrived(x_rcv.at[i], "X", i)
        k = (2 * h + i) % 4
        th, tl = split(d_buf[i] + c_rcv[i] + x_rcv[i])
        term = dot3(th, tl, rh[k], rl[k], NN)
        if i == 0:
            rot[...] = term
        else:
            rot[...] += term

    arrived(bias, "BI")
    arrived(m1, "M1")
    arrived(m2, "M2")
    biases = jnp.where(home, bias_mine[...], bias[...])
    one_over = 1.0 / biases
    scale_one, scale_two = one_over[0:1, 0:1], one_over[1:2, 0:1]

    @pl.loop(0, 8)
    def _(i):
        rows = pl.ds(pl.multiple_of(i * 32, 32), 32)
        value = rot[rows, :]
        first_new = BETA_ONE * m1[rows, :] + (1.0 - BETA_ONE) * value
        second_new = BETA_TWO * m2[rows, :] + (1.0 - BETA_TWO) * value * value
        direction = (first_new * scale_one) / (jnp.sqrt(second_new * scale_two) + EPSILON)
        high, low = split(direction)
        dh[rows, :] = high
        dl[rows, :] = low

    for j, (start, width) in enumerate(CUTS):
        rows = slice(start % Q, start % Q + width)
        u_all[j][q] = dot3(dh[...], dl[...], rh[start // Q, rows, :], rl[start // Q, rows, :], NT)
        mine = u_all[j].at[q]
        rcopy(mine, mine, "UX", across, j).start()
        rcopy(mine, mine, "US", sib, j).start()

    norm_b[...] = jnp.zeros_like(norm_b)
    zc = z * 2 + c
    xy = x * 4 + y
    for j, (start, width) in enumerate(CUTS):
        cols = slice(start, start + width)
        theirs = u_all[j].at[q_xp]
        arrived(theirs, "UX", j)
        rcopy(theirs, theirs, "UF", sib, j).start()
        arrived(u_all[j].at[q_sib], "US", j)
        arrived(u_all[j].at[q_xps], "UF", j)
        uh, ul = split(u_all[j][...].reshape(1024, width))
        result = dot3(lh[...], ll[...], uh, ul, NN)
        square = result * result
        total = square[:, 0:128]
        for k in range(1, width // 128):
            total = total + square[:, k * 128:(k + 1) * 128]
        norm_b[...] += jnp.sum(total.reshape(32, 8, 128), axis=0)

        if j == len(CUTS) - 1:
            sa_v[...] = jnp.concatenate([norm_g[...], norm_b[0:4, :] + norm_b[4:8, :]], axis=0)

            @pl.loop(1, 16)
            def _(i):
                other = (zc + i) % 16
                rcopy(sa_v, sa_r.at[i - 1], "SA", dev(x, y, other // 2, other % 2)).start()

        for i in range(64):
            back[i, :, cols] = result[i * 4:(i + 1) * 4, :]

        @pl.loop(0, 64)
        def _(t):
            yo, zo, co = (y + t // 16) % 4, (z + 3 * (t // 2)) % 8, (c + t) % 2
            o = (yo * 8 + zo) * 2 + co
            is_self = jnp.logical_and(home, t == 0)

            @pl.when(is_self)
            def _():
                pltpu.make_async_copy(back.at[o, :, cols], recv_o.at[slot, :, cols], sem(rsem, "O")).start()

            @pl.when(jnp.logical_not(is_self))
            def _():
                rcopy(back.at[o, :, cols], recv_o.at[slot, :, cols], "O", dev(q, yo, zo, co)).start()

        if 1 <= j <= 2:
            part = pl.ds((j - 1) * 128, 128)
            fetch(rot.at[part], rot_out.at[0, part], "RO")

    arrived(sa_r, "SA")
    sb_v[...] = sa_v[...] + jnp.sum(sa_r[...], axis=0)

    @pl.loop(1, 16)
    def _(i):
        other = (xy + i) % 16
        rcopy(sb_v, sb_r.at[i - 1], "SB", dev(other // 4, other % 4, z, c)).start()

    arrived(sb_r, "SB")
    totals = sb_v[...] + jnp.sum(sb_r[...], axis=0)
    grad_total = jnp.sum(totals[0:4, :], keepdims=True)
    back_total = jnp.sum(totals[4:8, :], keepdims=True)
    graft = jnp.sqrt(grad_total / back_total)
    graft_out[...] = jnp.broadcast_to(graft, (8, 128))
    arrived(recv_o, "O")
    arrived(rot, "RO")

    sent(sa_r, "SA")
    sent(sb_r, "SB")
    sent(bias, "BI")
    sent(rf.at[0], "RS")
    sent(rf.at[0], "RX")
    sent(rf.at[0], "RF")
    for j in range(NC):
        sent(a_snd.at[j], "A", j)
        sent(b_buf.at[j], "X", j)
        sent(c_snd.at[j], "C", j)
    for j in range(len(CUTS)):
        for name in ("US", "UX", "UF"):
            sent(u_all[j].at[0], name, j)

    @pl.when(home)
    def _():
        for g in range(NG):
            sent(recv_g.at[pl.ds(0, PER), pl.ds(0, 63)], "G", g)
        sent(recv_o.at[pl.ds(0, 63)], "O")

    @pl.when(away)
    def _():
        for g in range(NG):
            sent(recv_g.at[pl.ds(0, PER)], "G", g)
        sent(recv_o, "O")
        sent(lf, "L")
        sent(rf.at[0], "R")
        sent(m1, "M1")
        sent(m2, "M2")
        sent(rot, "RO")


def finish(
    owner, graft, received, rot_in, first_in, second_in, update, first_out, second_out,
    wire, rot, first, second, n1, n2, sin, sout,
):
    parts = 4
    size = Q // parts
    slots = 64 // parts
    copy = pltpu.make_async_copy

    def pieces(p):
        rows = pl.ds(p * size, size)
        return [
            copy(src.at[0, rows], dst.at[rows], sin.at[p, k])
            for k, (src, dst) in enumerate(((rot_in, rot), (first_in, first), (second_in, second)))
        ]

    def results(p):
        rows = pl.ds(p * size, size)
        return [
            copy(src.at[rows], dst.at[0, rows], sout.at[p, k])
            for k, (src, dst) in enumerate(((n1, first_out), (n2, second_out)))
        ]

    def incoming(p):
        some = pl.ds(p * slots, slots)
        return copy(received.at[some], wire.at[some], sin.at[p, 3])

    for p in range(parts):
        for piece in pieces(p):
            piece.start()
    for p in range(parts):
        incoming(p).start()
    for p in range(parts):
        for piece in pieces(p):
            piece.wait()
        rows = pl.ds(p * size, size)
        value = rot[rows, :]
        n1[rows, :] = BETA_ONE * first[rows, :] + (1.0 - BETA_ONE) * value
        n2[rows, :] = BETA_TWO * second[rows, :] + (1.0 - BETA_TWO) * value * value
        for result in results(p):
            result.start()
    scale = graft[0:1, 0:1]
    for p in range(parts):
        incoming(p).wait()

        @pl.loop(0, slots, unroll=4)
        def _(i):
            o = p * slots + i
            wire[o] = wire[o] * scale
            copy(wire.at[o], update.at[owner[o]], sout.at[parts, 0]).start()

    for p in range(parts):
        for result in results(p):
            result.wait()
    copy(wire, update, sout.at[parts, 0]).wait()


def body(gradient, owner_table, restart_steps, left_basis, right_basis, first_moment, second_moment):
    vmem = pl.BlockSpec(memory_space=pltpu.VMEM)
    smem = pl.BlockSpec(memory_space=pltpu.SMEM)
    anywhere = pl.BlockSpec(memory_space=pl.ANY)
    rows_f = pltpu.VMEM((Q, 1024), F32)
    rows_b = pltpu.VMEM((Q, 1024), BF16)
    wire = pltpu.VMEM((64, 4, 1024), F32)
    chunks = pltpu.VMEM((NC, Q, W), F32)
    chunks_b = pltpu.VMEM((NC, Q, W), BF16)
    tile = pltpu.VMEM((8, 128), F32)
    lt = pltpu.VMEM((4, Q, Q), BF16)
    whole_b = pltpu.VMEM((4, Q, 1024), BF16)
    fifteen = pltpu.VMEM((15, 8, 128), F32)
    received, rotated, graft = pl.pallas_call(
        kernel,
        out_shape=(
            jax.ShapeDtypeStruct((64, 4, 1024), F32),
            jax.ShapeDtypeStruct((1, Q, 1024), F32),
            jax.ShapeDtypeStruct((8, 128), F32),
        ),
        in_specs=[smem, smem, anywhere, anywhere, anywhere, anywhere, anywhere],
        out_specs=(anywhere, anywhere, vmem),
        scratch_shapes=[
            wire, pltpu.VMEM((64, NC, 4, W), F32), pltpu.VMEM((NC, 64, 4, W), F32),
            chunks_b, chunks_b, rows_f, rows_b, rows_b, lt, lt,
            pltpu.VMEM((4, Q, 1024), F32), whole_b, whole_b,
            chunks, chunks, chunks, chunks, chunks, chunks, chunks,
            rows_f, rows_f, rows_f, rows_b, rows_b,
            *(pltpu.VMEM((4, Q, width), F32) for _, width in CUTS), wire,
            tile, tile, tile, fifteen, tile, fifteen,
            pltpu.VMEM((4, 128), F32), tile,
            pltpu.SemaphoreType.DMA((N_SEMS,)),
            pltpu.SemaphoreType.DMA((N_SEMS,)),
            pltpu.SemaphoreType.REGULAR((3,)),
        ],
        compiler_params=pltpu.CompilerParams(
            collective_id=0, has_side_effects=True, vmem_limit_bytes=56 * 1024 * 1024
        ),
    )(owner_table, restart_steps, gradient, left_basis, right_basis, first_moment, second_moment)

    return pl.pallas_call(
        finish,
        out_shape=(
            jax.ShapeDtypeStruct((64, 4, 1024), F32),
            jax.ShapeDtypeStruct((1, Q, 1024), F32),
            jax.ShapeDtypeStruct((1, Q, 1024), F32),
        ),
        in_specs=[smem, vmem, anywhere, anywhere, anywhere, anywhere],
        out_specs=(anywhere, anywhere, anywhere),
        scratch_shapes=[
            wire, rows_f, rows_f, rows_f, rows_f, rows_f,
            pltpu.SemaphoreType.DMA((4, 4)), pltpu.SemaphoreType.DMA((5, 2)),
        ],
        compiler_params=pltpu.CompilerParams(vmem_limit_bytes=56 * 1024 * 1024),
    )(owner_table, graft, received, rotated, first_moment, second_moment)


def solution(mesh):
    in_specs = (
        P(None, ("shard", "blk"), None),
        P(),
        P("blk"),
        P("blk", "shard", None),
        P("blk", "shard", None),
        P("blk", "shard", None),
        P("blk", "shard", None),
    )
    out_specs = (P(None, ("shard", "blk"), None), P("blk", "shard", None), P("blk", "shard", None))
    return jax.shard_map(body, mesh=mesh, in_specs=in_specs, out_specs=out_specs, check_vma=False)
```
